32 devices in a mesh: groups: 2 (over y), bx: 4 (over z), by: 2 (over x), bz: 2 (over core).
Axes of the slice: x: 2, y: 2, z: 4, core: 2. Of those that a mesh axis runs over, the one named last changes fastest.
Arguments:
- slab: float32 [4, 512, 1024], P(('groups', 'bz'), 'bx', 'by'), parts along dimension 0, may hold values from -6 to 6
- plane_test: float32 [2, 256], P('bz'), may hold values from -4 to 4
- row_test: float32 [512, 256], P('bx'), may hold values from -0.25 to 0.25
- col_test: float32 [1024, 256], P('by'), may hold values from -0.1875 to 0.1875
- core_planes: float32 [512, 2], P('bz'), may hold values from -4 to 4
- core_rows: float32 [512, 512], P(None, 'bx'), may hold values from -0.25 to 0.25
- core_cols: float32 [512, 1024], P(None, 'by'), may hold values from -0.1875 to 0.1875
Outputs:
- plane_sketch: float32 [4, 256], P(('groups', 'bz')), parts along dimension 0
- row_sketch: float32 [1024, 256], P(('groups', 'bx'), ('by', 'bz')), parts along dimension 0
- col_sketch: float32 [2048, 256], P(('groups', 'by'), ('bx', 'bz')), parts along dimension 0
- core_sketch: float32 [1024, 512, 512], P(('groups', 'bz'), 'bx', 'by'), parts along dimension 0
The draws below stay inside these ranges and needn't reach their ends.
There are 2 independent parts, one for each index of `groups`. The reference program is written for one: setup_inputs(seed, part) draws one part's arguments, and reference() takes and returns one part's arrays. A program takes and returns all parts, laid end to end along the dimension named above; an argument that names none is the same for every part. Nothing has to cross between parts.
All inputs are finite; a program needn't handle non-finite values.
Results may differ from the reference program's by a relative error of at most 0.00011.
Values sent between devices are 32-bit elements; how exact they have to be, the bound alone decides.
No kernel may reach another device: no remote copies, remote signals or barrier semaphores. Data moves between devices by JAX's collectives and lax.ppermute only.
A program may use at most 128 MiB of HBM per device.

```python
import jax
import jax.numpy as jnp
from jax import lax

S = 512
K = 256
P_SIZE = 2
NR = 512
NC = 1024


def shard_levels(own_key, dims, pieces, smallest, top_value):
    level = 1.0
    for position, shards_of in pieces:
        heights = jax.random.uniform(jax.random.fold_in(jax.random.fold_in(own_key, 6), position), (shards_of,), jnp.float32, smallest / len(pieces), top_value / len(pieces))
        level = level * jnp.repeat(jnp.exp(heights), dims[position] // shards_of).reshape((-1,) + (1,) * (len(dims) - 1 - position))
    return level


def centred(rng, dims, spread, most, pieces=(), held_as=jnp.bfloat16):
    array = spread * jax.random.normal(rng, dims, jnp.float32)
    if pieces:
        array = array * shard_levels(rng, dims, pieces, -0.22, 0.18)
    return jnp.clip(array, -most, most).astype(held_as)


def setup_inputs(seed: int = 0, part: int = 0) -> dict:
    keys = jax.random.split(jax.random.key(seed), 8)
    part_keys = jax.random.split(jax.random.fold_in(keys[7], part), 8)
    return {
        "slab": centred(part_keys[0], (P_SIZE, NR, NC), 1.0, 6.0, ((0, 2), (1, 4), (2, 2)), jnp.float32),
        "plane_test": centred(keys[1], (P_SIZE, K), P_SIZE ** -0.5, 4.0, ((0, 2),), jnp.float32),
        "row_test": centred(keys[2], (NR, K), NR ** -0.5, 0.25, ((0, 4),), jnp.float32),
        "col_test": centred(keys[3], (NC, K), NC ** -0.5, 0.1875, ((0, 2),), jnp.float32),
        "core_planes": centred(keys[4], (S, P_SIZE), P_SIZE ** -0.5, 4.0, ((0, 2),), jnp.float32),
        "core_rows": centred(keys[5], (S, NR), NR ** -0.5, 0.25, ((1, 4),), jnp.float32),
        "core_cols": centred(keys[6], (S, NC), NC ** -0.5, 0.1875, ((1, 2),), jnp.float32),
    }


def reference(slab, plane_test, row_test, col_test, core_planes, core_rows, core_cols):
    highest = lax.Precision.HIGHEST
    by_col = jnp.einsum('pij,jr->pir', slab, col_test, precision=highest)
    plane_sketch = jnp.einsum('pir,ir->pr', by_col, row_test, precision=highest)
    row_sketch = jnp.einsum('pir,pr->ir', by_col, plane_test, precision=highest)
    by_row = jnp.einsum('pij,ir->pjr', slab, row_test, precision=highest)
    col_sketch = jnp.einsum('pjr,pr->jr', by_row, plane_test, precision=highest)
    shrunk = jnp.einsum('pij,bj->pib', slab, core_cols, precision=highest)
    partial_value = jnp.einsum('pib,ai->pab', shrunk, core_rows, precision=highest)
    core_sketch = jnp.einsum('cp,pab->cab', core_planes, partial_value, precision=highest)
    return plane_sketch, row_sketch, col_sketch, core_sketch
```

```python
import functools

import jax
import jax.numpy as jnp
from jax import lax
from jax.experimental import pallas as pl
from jax.experimental.pallas import tpu as pltpu
from jax.sharding import PartitionSpec as P

F32 = jnp.float32
VMEM_LIMIT = 40 << 20
PIECES = (4, 4)


def split(x):
    hi = x.astype(jnp.bfloat16)
    return hi, (x - hi.astype(F32)).astype(jnp.bfloat16)


def dot3(a, b, contract):
    dims = ((contract[:1], contract[1:]), ((), ()))
    (ah, al), (bh, bl) = split(a), split(b)
    dot = functools.partial(lax.dot_general, dimension_numbers=dims, preferred_element_type=F32)
    return dot(ah, bh) + (dot(ah, bl) + dot(al, bh))


def call(kernel, outs, operands, spaces, out_spaces=None, scratch=(), cost=None, **kw):
    vmem = pl.BlockSpec(memory_space=pltpu.VMEM)
    spec = {"v": vmem, "s": pl.BlockSpec(memory_space=pltpu.SMEM), "a": pl.BlockSpec(memory_space=pl.ANY)}
    out_spaces = out_spaces or "v" * len(outs)
    return pl.pallas_call(
        kernel,
        out_shape=[jax.ShapeDtypeStruct(s, F32) for s in outs],
        in_specs=[spec[s] for s in spaces],
        out_specs=[spec[s] for s in out_spaces],
        scratch_shapes=list(scratch),
        cost_estimate=cost and pl.CostEstimate(flops=cost[0], bytes_accessed=cost[1], transcendentals=0),
        compiler_params=pltpu.CompilerParams(vmem_limit_bytes=VMEM_LIMIT),
        **kw,
    )(*operands)


def pairs(n, k):
    return [(i, i ^ k) for i in range(n)]


def shrink_others(n, slab, cols, *refs):
    outs, (s_buf, c_buf, sem) = refs[: n - 1], refs[n - 1 :]
    me = lax.axis_index("by")
    bb = c_buf.shape[1]
    first = pltpu.make_async_copy(slab.at[0], s_buf, sem.at[n - 1])
    first.start()
    copies = []
    for k in range(1, n):
        start = pl.multiple_of((me ^ k) * bb, bb)
        copies.append(pltpu.make_async_copy(cols.at[pl.ds(start, bb)], c_buf.at[k - 1], sem.at[k - 1]))
        copies[-1].start()
    first.wait()
    for k in range(1, n):
        copies[k - 1].wait()
        outs[k - 1][...] = dot3(s_buf[...], c_buf[k - 1], (1, 1))


def local_terms(nbx, nby, nbz, slab, cols, row_test, col_test, plane_test, own, packed, plane, c_buf, sem):
    me = lax.axis_index("by")
    bb = c_buf.shape[0]
    copy = pltpu.make_async_copy(cols.at[pl.ds(pl.multiple_of(me * bb, bb), bb)], c_buf, sem)
    copy.start()
    brick = slab[0]
    nj = brick.shape[1]
    by_row = dot3((row_test[...] * plane_test[...]).T, brick, (1, 0))
    rb = by_row.shape[0] // (nbx * nbz)
    for x in range(nbx):
        for z in range(nbz):
            packed[z, x * rb : (x + 1) * rb, :nj] = by_row[(x * nbz + z) * rb : (x * nbz + z + 1) * rb]
    by_col = dot3(brick, col_test[...], (1, 0))
    total = jnp.sum(by_col * row_test[...], axis=0, keepdims=True)
    plane[...] = jnp.broadcast_to(total, plane.shape)
    by_col = (by_col * plane_test[...]).T
    rb = by_col.shape[0] // (nby * nbz)
    for y in range(nby):
        for z in range(nbz):
            packed[z, y * rb : (y + 1) * rb, nj:] = by_col[(y * nbz + z) * rb : (y * nbz + z + 1) * rb]
    copy.wait()
    own[...] = dot3(brick, c_buf[...], (1, 1))


def core_terms(n, cuts, rows, own, *refs):
    received, outs = refs[: -1 - (n - 1) * (len(cuts) - 1)], refs[-1 - (n - 1) * (len(cuts) - 1) :]
    me = lax.axis_index("bx")
    ab = rows.shape[0] // n
    reduced = own[...]
    for r in received:
        reduced = reduced + r[...]
    hi, lo = split(reduced)
    right = jnp.concatenate([hi, hi, lo], axis=0)

    def block(start, size):
        hi, lo = split(rows[pl.ds(pl.multiple_of(start, 8), size), :])
        left = jnp.concatenate([hi, lo, hi], axis=1)
        return lax.dot_general(left, right, (((1,), (0,)), ((), ())), preferred_element_type=F32)

    at = 1
    for lo_row, hi_row in zip(cuts[:-1], cuts[1:]):
        for k in range(1, n):
            outs[at][...] = block((me ^ k) * ab + lo_row, hi_row - lo_row)
            at += 1
    outs[0][...] = block(me * ab, ab)


def add_all(lo, own, *refs):
    *received, out = refs
    total = own[lo : lo + out.shape[0]]
    for r in received:
        total = total + r[...]
    out[...] = total


def split_sketches(nbx, nby, nj, packed, received, plane, *refs):
    row_own, col_own = refs[0], refs[1]
    row_out, col_out = refs[2 : 1 + nby], refs[1 + nby :]
    z, y, x = lax.axis_index("bz"), lax.axis_index("by"), lax.axis_index("bx")
    rb, cb, ni = row_own.shape[0], col_own.shape[0], row_own.shape[1]

    def row_block(d):
        at = pl.ds(pl.multiple_of(d * rb, 8), rb)
        return packed[z, at, nj:] + received[at, nj:]

    def col_block(d):
        at = pl.ds(pl.multiple_of(d * cb, 8), cb)
        return packed[z, at, :nj] + received[at, :nj]

    row_own[...] = row_block(y)
    col_own[...] = col_block(x)
    for k in range(1, nby):
        row_out[k - 1][:rb] = row_block(y ^ k)
        for part in range(plane.shape[1] // ni):
            row_out[k - 1][rb + 8 * part : rb + 8 * (part + 1)] = plane[:, part * ni : (part + 1) * ni]
    for k in range(1, nbx):
        col_out[k - 1][...] = col_block(x ^ k)


def write_core(at, cb, nb, me, planes, own, other, *refs):
    out, buf, sem = refs[-3:]
    me = lax.axis_index("bz")
    rows = own.shape[0]
    steps = out.shape[0] // cb

    def copy(s, slot):
        return pltpu.make_async_copy(buf.at[slot], out.at[pl.ds(s * cb, cb), pl.ds(at, rows)], sem.at[slot])

    def step(s, _):
        slot = lax.rem(s, nb)

        @pl.when(s >= nb)
        def _():
            copy(s - nb, slot).wait()

        for c in range(cb):
            buf[slot, c] = planes[me, s * cb + c] * own[...] + planes[1 - me, s * cb + c] * other[...]
        copy(s, slot).start()
        return 0

    lax.fori_loop(0, steps, step, 0)

    def drain(s, _):
        copy(s, lax.rem(s, nb)).wait()
        return 0

    lax.fori_loop(steps - nb, steps, drain, 0)


def finish(nbx, nby, plane, *refs):
    row_own, col_own = refs[0], refs[1]
    row_in, col_in, plane_in = refs[2 : 1 + nby], refs[1 + nby : nby + nbx], refs[nby + nbx : nby + 2 * nbx - 1]
    plane_out, row_out, col_out = refs[nby + 2 * nbx - 1 :]
    rb = row_own.shape[0]
    row, col = row_own[...], col_own[...]
    for r in row_in:
        row = row + r[:rb]
    for r in col_in:
        col = col + r[...]
    total = plane[:1]
    for r in plane_in:
        total = total + r[:1]
    plane_out[...] = total
    row_out[...] = row.T
    col_out[...] = col.T


def direct(mesh, slab, plane_test, row_test, col_test, core_planes, core_rows, core_cols):
    nbx, nby, nbz = mesh.shape["bx"], mesh.shape["by"], mesh.shape["bz"]
    _, ni, nj = slab.shape
    k = row_test.shape[1]
    ab, bb = core_rows.shape[0] // nbx, core_cols.shape[0] // nby
    nc = core_planes.shape[0]
    rb, cb = k // (nby * nbz), k // (nbx * nbz)
    cuts = [0]
    for p in PIECES:
        cuts.append(cuts[-1] + p * ab // sum(PIECES))

    outs = call(
        functools.partial(shrink_others, nby),
        [(ni, bb)] * (nby - 1),
        (slab, core_cols),
        "aa",
        scratch=[pltpu.VMEM((ni, nj), F32), pltpu.VMEM((nby - 1, bb, nj), F32), pltpu.SemaphoreType.DMA((nby,))],
        cost=(6 * ni * bb * nj * (nby - 1), 4 * (ni * nj + bb * nj)),
    )
    shrunk_in = [lax.ppermute(o, "by", pairs(nby, i)) for i, o in enumerate(outs, 1)]

    own, packed, plane = call(
        functools.partial(local_terms, nbx, nby, nbz),
        [(ni, bb), (nbz, k // nbz, nj + ni), (8, k)],
        (slab, core_cols, row_test, col_test, plane_test),
        "vavvv",
        scratch=[pltpu.VMEM((bb, nj), F32), pltpu.SemaphoreType.DMA],
        cost=(6 * ni * nj * (bb + 2 * k), 4 * (ni * nj + bb * nj + nj * k)),
    )
    z = lax.axis_index("bz")
    packed_in = lax.ppermute(lax.dynamic_index_in_dim(packed, 1 - z, 0, False), "bz", pairs(nbz, 1))

    outs = call(
        functools.partial(core_terms, nbx, cuts),
        [(ab, bb)] + [(hi - lo, bb) for lo, hi in zip(cuts[:-1], cuts[1:]) for _ in range(nbx - 1)],
        (core_rows, own, *shrunk_in),
        "vv" + "v" * (nby - 1),
        cost=(6 * ni * bb * core_rows.shape[0], 4 * core_rows.size),
    )
    core_own, sends = outs[0], outs[1:]
    arrivals = [
        [lax.ppermute(sends[p * (nbx - 1) + i - 1], "bx", pairs(nbx, i)) for i in range(1, nbx)]
        for p in range(len(PIECES))
    ]

    outs = call(
        functools.partial(split_sketches, nbx, nby, nj),
        [(rb, ni), (cb, nj)] + [(rb + 8 * (k // ni), ni)] * (nby - 1) + [(cb, nj)] * (nbx - 1),
        (packed, packed_in, plane),
        "vvv",
    )
    row_own, col_own, row_send, col_send = outs[0], outs[1], outs[2 : 1 + nby], outs[1 + nby :]
    row_in = [lax.ppermute(o, "by", pairs(nby, i)) for i, o in enumerate(row_send, 1)]
    for r in row_in:
        plane = plane + r[rb:].reshape(k // ni, 8, ni).transpose(1, 0, 2).reshape(8, k)
    plane_in = [lax.ppermute(plane, "bx", pairs(nbx, i)) for i in range(1, nbx)]
    col_in = [lax.ppermute(o, "bx", pairs(nbx, i)) for i, o in enumerate(col_send, 1)]

    planes = core_planes.T
    core = None
    for p, (lo, hi) in enumerate(zip(cuts[:-1], cuts[1:])):
        (total,) = call(
            functools.partial(add_all, lo), [(hi - lo, bb)], (core_own, *arrivals[p]), "v" * nbx
        )
        other = lax.ppermute(total, "bz", pairs(nbz, 1))
        more = {} if core is None else {"input_output_aliases": {3: 0}}
        extra = () if core is None else (core,)
        (core,) = call(
            functools.partial(write_core, lo, 8, 8, None),
            [(nc, ab, bb)],
            (planes, total, other, *extra),
            "svv" + "a" * len(extra),
            "a",
            scratch=[pltpu.VMEM((8, 8, hi - lo, bb), F32), pltpu.SemaphoreType.DMA((8,))],
            cost=(3 * nc * (hi - lo) * bb, 4 * nc * (hi - lo) * bb),
            **more,
        )
    plane_sketch, row_sketch, col_sketch = call(
        functools.partial(finish, nbx, nby),
        [(1, k), (ni, rb), (nj, cb)],
        (plane, row_own, col_own, *row_in, *col_in, *plane_in),
        "v" * (3 + nby - 1 + 2 * (nbx - 1)),
    )
    return plane_sketch, row_sketch, col_sketch, core


def stepwise(slab, plane_test, row_test, col_test, core_planes, core_rows, core_cols):
    einsum = functools.partial(jnp.einsum, precision=lax.Precision.HIGHEST)
    by_col = einsum("pij,jr->pir", slab, col_test)
    plane_part = einsum("pir,ir->pr", by_col, row_test)
    row_part = einsum("pir,pr->ir", by_col, plane_test)
    by_row = einsum("pij,ir->pjr", slab, row_test)
    col_part = einsum("pjr,pr->jr", by_row, plane_test)
    plane_sketch = lax.psum(plane_part, ("bx", "by"))
    row_sketch = lax.psum_scatter(row_part, ("by", "bz"), scatter_dimension=1, tiled=True)
    col_sketch = lax.psum_scatter(col_part, ("bx", "bz"), scatter_dimension=1, tiled=True)
    shrunk = einsum("pij,bj->pib", slab, core_cols)
    reduced = lax.psum_scatter(shrunk, "by", scatter_dimension=2, tiled=True)
    partial_value = einsum("pib,ai->pab", reduced, core_rows)
    partial_value = lax.psum_scatter(partial_value, "bx", scatter_dimension=1, tiled=True)
    both = lax.all_gather(partial_value, "bz", axis=0, tiled=True)
    core_sketch = einsum("cp,pab->cab", core_planes, both)
    return plane_sketch, row_sketch, col_sketch, core_sketch


def solution(mesh):
    in_specs = (
        P(("groups", "bz"), "bx", "by"),
        P("bz", None),
        P("bx", None),
        P("by", None),
        P("bz", None),
        P(None, "bx"),
        P(None, "by"),
    )
    out_specs = (
        P(("groups", "bz"), None),
        P(("groups", "bx"), ("by", "bz")),
        P(("groups", "by"), ("bx", "bz")),
        P(("groups", "bz"), "bx", "by"),
    )
    short = mesh.shape["bx"] in (2, 4) and mesh.shape["by"] in (2, 4) and mesh.shape["bz"] == 2
    body = functools.partial(direct, mesh) if short else stepwise
    return jax.shard_map(body, mesh=mesh, in_specs=in_specs, out_specs=out_specs, check_vma=False)
```

```python
import functools

import jax
import jax.numpy as jnp
from jax import lax
from jax.experimental import pallas as pl
from jax.experimental.pallas import tpu as pltpu
from jax.sharding import PartitionSpec as P

F32 = jnp.float32
BF16 = jnp.bfloat16
VMEM_LIMIT = 40 << 20
DIRECT = (4, 2, 2)
FIRST = 5
FIRST_ORDER = (2, 1, 3)
SECOND_ORDER = (1, 2, 3)


def split(x):
    hi = x.astype(BF16)
    return hi, (x - hi.astype(F32)).astype(BF16)


def dot(a, b, contract):
    dims = ((contract[:1], contract[1:]), ((), ()))
    return lax.dot_general(a, b, dims, preferred_element_type=F32)


def rows_dot(a, b):
    m, n = a[0].shape[0], b[0].shape[0]
    r = dot(jnp.concatenate(a), jnp.concatenate(b), (1, 1))
    return r[:m, :n] + (r[:m, n:] + r[m:, :n])


def call(kernel, outs, operands, spaces, out_spaces=None, scratch=(), cost=None, **kw):
    spec = {
        "v": pl.BlockSpec(memory_space=pltpu.VMEM),
        "h": pl.BlockSpec(memory_space=pltpu.HBM),
    }
    out_spaces = out_spaces or "v" * len(outs)
    operands = [
        pltpu.with_memory_space_constraint(o, pltpu.HBM) if s == "h" else o for o, s in zip(operands, spaces)
    ]
    return pl.pallas_call(
        kernel,
        out_shape=[s if hasattr(s, "dtype") else jax.ShapeDtypeStruct(s, F32) for s in outs],
        in_specs=[spec[s] for s in spaces],
        out_specs=[spec[s] for s in out_spaces],
        scratch_shapes=list(scratch),
        cost_estimate=cost and pl.CostEstimate(flops=cost[0], bytes_accessed=cost[1], transcendentals=0),
        compiler_params=pltpu.CompilerParams(vmem_limit_bytes=VMEM_LIMIT),
        **kw,
    )(*operands)


def pairs(n, k):
    return [(i, i ^ k) for i in range(n)]


def block(i, size):
    return pl.ds(pl.multiple_of(i * size, size), size)


def read(sources, buffers, sem):
    copies = [pltpu.make_async_copy(s, b, sem.at[i]) for i, (s, b) in enumerate(zip(sources, buffers))]
    for c in copies:
        c.start()
    return copies


def others_columns(slab, cols, send, s_buf, c_buf, sem):
    other = 1 - lax.axis_index("by")
    bb = send.shape[0]
    copies = read((slab.at[0], cols.at[block(other, bb)]), (s_buf, c_buf), sem)
    copies[0].wait()
    brick = split(s_buf[...])
    copies[1].wait()
    send[...] = rows_dot(split(c_buf[...]), brick)


def own_terms(slab, cols, col_test, row_test, plane_test, core_rows, after, *refs):
    own, row_own, row_away, plane_own, col_own, col_away, left, *bufs, sem = refs
    y, z = lax.axis_index("by"), lax.axis_index("bz")
    s_buf, rt_buf, pt_buf, ct_buf, c_buf, cr_buf = bufs
    bb, ni = own.shape
    copies = read((slab.at[0], row_test, plane_test, col_test, cols.at[block(y, bb)], core_rows), bufs, sem)
    for c in copies[:3]:
        c.wait()
    brick = split(s_buf[...])
    both = jnp.concatenate(brick)
    k = rt_buf.shape[1]
    hi, lo = split((rt_buf[...] * pt_buf[...]).T)
    by_row = dot(jnp.concatenate([jnp.concatenate([hi, hi], axis=1), jnp.concatenate([lo, lo], axis=1)]), both, (1, 0))
    by_row = by_row[:k] + by_row[k:]
    cb = col_own.shape[0] // 4
    for d in range(4):
        at = 2 * d * cb
        low, high = by_row[at : at + cb], by_row[at + cb : at + 2 * cb]
        col_own[d * cb : (d + 1) * cb] = jnp.where(z == 0, low, high)
        col_away[d * cb : (d + 1) * cb] = jnp.where(z == 0, high, low)
    copies[3].wait()
    hi, lo = split(ct_buf[...])
    by_col = dot(both, hi, (1, 0))
    by_col = by_col[:ni] + (by_col[ni:] + dot(brick[0], lo, (1, 0)))
    plane = jnp.sum(by_col * rt_buf[...], axis=0, keepdims=True)
    plane_own[...] = jnp.broadcast_to(plane, plane_own.shape)
    turned = (by_col * pt_buf[...]).T
    rows = row_own.shape[0]
    low, high = turned[:rows], turned[rows:]
    row_own[...] = jnp.where(y == 0, low, high)
    row_away[...] = jnp.where(y == 0, high, low)
    copies[4].wait()
    own[...] = rows_dot(split(c_buf[...]), brick)
    copies[5].wait()
    hi, lo = split(cr_buf[...])
    left[:, :ni] = hi
    left[:, ni : 2 * ni] = lo
    left[:, 2 * ni :] = hi


def core_first(left, own, received, plane, right, *outs):
    x = lax.axis_index("bx")
    ni = own.shape[1]
    hi, lo = split(own[...] + received[...])
    right[:, :ni] = hi
    right[:, ni : 2 * ni] = hi
    right[:, 2 * ni :] = lo
    ab = left.shape[0] // 4
    for k, out in zip(FIRST_ORDER, outs):
        cut = out.shape[0] - 8
        rows = pl.ds(pl.multiple_of((x ^ k) * ab, ab), cut)
        out[:cut] = dot(left[rows], right[...], (1, 1))
        out[cut:] = plane[...]


def core_second(cut, left, right, col_terms, col_received, planes, *refs):
    core_own, col_own, table, *outs, p_buf, sem = refs
    copy = pltpu.make_async_copy(planes, p_buf, sem)
    copy.start()
    x, z = lax.axis_index("bx"), lax.axis_index("bz")
    ab = left.shape[0] // 4
    rest = ab - cut
    cb, wide = col_own.shape[0], core_own.shape[1]
    for k, out in zip(SECOND_ORDER, outs):
        rows = pl.ds(pl.multiple_of((x ^ k) * ab + cut, 16), rest)
        out[:rest] = dot(left[rows], right[...], (1, 1))
        col = col_terms[block(x ^ k, cb)] + col_received[block(x ^ k, cb)]
        for part in range(col.shape[1] // wide):
            out[rest + part * cb : rest + (part + 1) * cb] = col[:, part * wide : (part + 1) * wide]
    col_own[...] = col_terms[block(x, cb)] + col_received[block(x, cb)]
    core_own[...] = dot(left[block(x, ab)], right[...], (1, 1))
    copy.wait()
    for i, p in enumerate((z, 1 - z)):
        table[i] = jnp.broadcast_to(p_buf[pl.ds(p, 1), :], table.shape[:0:-1]).T


def sum_first(core_own, row_away, plane_own, in_a, in_b, in_c, out, x_send, plane_sum):
    cut, rows = out.shape[0], row_away.shape[0]
    ni = row_away.shape[1]
    out[...] = (core_own[:cut] + in_a[:cut]) + (in_b[:cut] + in_c[:cut])
    plane = (plane_own[...] + in_a[cut:]) + (in_b[cut:] + in_c[cut:])
    rows8 = lax.broadcasted_iota(jnp.int32, plane_sum.shape, 0)
    plane = jnp.where(rows8 == 0, plane[:, :ni], plane[:, ni:])
    plane_sum[...] = plane
    x_send[:rows] = row_away[...]
    x_send[rows:] = plane


def sum_second(core_own, row_own, plane_sum, col_own, x_received, in_a, in_b, in_c, core, out, row_mine, plane, col):
    z = lax.axis_index("bz")
    rows, ni = row_own.shape
    rb, cb = rows // 2, col_own.shape[0]
    rest = in_a.shape[0] - col_own.shape[1] // out.shape[1] * cb
    out[:rest] = (core_own[core_own.shape[0] - rest :] + in_a[:rest]) + (in_b[:rest] + in_c[:rest])
    mine, away = block(z, rb), block(1 - z, rb)
    row_mine[...] = row_own[mine] + x_received[mine]
    turned = row_own[away] + x_received[away]
    out[rest:, :ni] = turned[: rb // 2]
    out[rest:, ni:] = turned[rb // 2 :]
    total = plane_sum[...] + x_received[rows:]
    for part in range(plane.shape[1] // ni):
        plane[:, part * ni : (part + 1) * ni] = total[part : part + 1]
    wide = out.shape[1]
    for part in range(col.shape[1] // wide):
        lanes = slice(part * wide, (part + 1) * wide)
        got = slice(rest + part * cb, rest + (part + 1) * cb)
        col[:, lanes] = (col_own[:, lanes] + in_a[got]) + (in_b[got] + in_c[got])


def write(at, own, other, table, out, buf, sem):
    nb, cb, rows = buf.shape[:3]
    steps = out.shape[0] // cb

    def copy(s, slot):
        return pltpu.make_async_copy(buf.at[slot], out.at[block(s, cb), pl.ds(at, rows)], sem.at[slot])

    def step(s, _):
        slot = lax.rem(s, nb)

        @pl.when(s >= nb)
        def _():
            copy(s - nb, slot).wait()

        for c in range(cb):
            row = pl.ds(s * cb + c, 1)
            buf[slot, c] = table[0, row] * own[:rows] + table[1, row] * other[:rows]
        copy(s, slot).start()
        return 0

    lax.fori_loop(0, steps, step, 0)

    def drain(s, _):
        copy(s, lax.rem(s, nb)).wait()
        return 0

    lax.fori_loop(steps - nb, steps, drain, 0)


def write_first(own, other, table, out, buf, sem):
    write(0, own, other, table, out, buf, sem)


def write_second(own, other, table, row_mine, plane, col, core, out, plane_out, row_out, col_out, buf, sem, row_buf, out_sem):
    rest, ni = buf.shape[2], row_buf.shape[1]
    half = row_buf.shape[0] // 2
    row_buf[:half] = row_mine[:half] + other[rest:, :ni]
    row_buf[half:] = row_mine[half:] + other[rest:, ni:]
    copies = read((plane, row_buf, col), (plane_out, row_out, col_out), out_sem)
    write(out.shape[1] - rest, own, other, table, out, buf, sem)
    for c in copies:
        c.wait()


def direct(mesh, slab, plane_test, row_test, col_test, core_planes, core_rows, core_cols):
    nbx, nby, nbz = DIRECT
    _, ni, nj = slab.shape
    k = row_test.shape[1]
    na, nc = core_rows.shape[0], core_planes.shape[0]
    ab, bb = na // nbx, core_cols.shape[0] // nby
    rb, cb = k // (nby * nbz), k // (nbx * nbz)
    cut = FIRST * ab // 8
    rest = ab - cut
    dma = pltpu.SemaphoreType.DMA

    (x_send,) = call(
        others_columns,
        [(bb, ni)],
        (slab, core_cols),
        "hh",
        scratch=[pltpu.VMEM((ni, nj), F32), pltpu.VMEM((bb, nj), F32), dma((2,))],
        cost=(6 * ni * nj * bb, 4 * (ni + bb) * nj),
    )
    x_in = lax.ppermute(x_send, "by", pairs(nby, 1))

    own, row_own, row_away, plane_own, col_terms, col_away, left = call(
        own_terms,
        [
            (bb, ni),
            (nbz * rb, ni),
            (nbz * rb, ni),
            (8, k),
            (nbx * cb, nj),
            (nbx * cb, nj),
            jax.ShapeDtypeStruct((na, 3 * ni), BF16),
        ],
        (slab, core_cols, col_test, row_test, plane_test, core_rows, x_send),
        "hhhhhhv",
        scratch=[
            pltpu.VMEM((ni, nj), F32),
            pltpu.VMEM((ni, k), F32),
            pltpu.VMEM((1, k), F32),
            pltpu.VMEM((nj, k), F32),
            pltpu.VMEM((bb, nj), F32),
            pltpu.VMEM((na, ni), F32),
            dma((6,)),
        ],
        cost=(6 * ni * nj * (bb + 2 * k), 4 * (ni * nj + bb * nj + nj * k)),
    )
    right, *sends = call(
        core_first,
        [jax.ShapeDtypeStruct((bb, 3 * ni), BF16)] + [(cut + 8, bb)] * 3,
        (left, own, x_in, plane_own),
        "vvvv",
        cost=(6 * ni * bb * 3 * cut, 4 * ni * bb),
    )
    col_away, *sends = lax.optimization_barrier((col_away, *sends))
    first_in = [lax.ppermute(s, "bx", pairs(nbx, i)) for i, s in zip(FIRST_ORDER, sends)]
    col_in = lax.ppermute(col_away, "bz", pairs(nbz, 1))

    core_own, col_own, table, *sends = call(
        functools.partial(core_second, cut),
        [(ab, bb), (cb, nj), (2, nc, bb)] + [(rest + cb * nj // bb, bb)] * 3,
        (left, right, col_terms, col_in, core_planes.T),
        "vvvvh",
        scratch=[pltpu.VMEM((nbz, nc), F32), dma],
        cost=(6 * ni * bb * 4 * ab, 4 * ni * bb),
    )
    second_in = [lax.ppermute(s, "bx", pairs(nbx, i)) for i, s in zip(SECOND_ORDER, sends)]

    first, x_send, plane_sum = call(
        sum_first,
        [(cut, bb), (nbz * rb + 8, ni), (8, ni)],
        (core_own, row_away, plane_own, *first_in),
        "vvvvvv",
    )
    first_other = lax.ppermute(first, "bz", pairs(nbz, 1))
    x_in = lax.ppermute(x_send, "by", pairs(nby, 1))
    (core,) = call(
        write_first,
        [(nc, ab, bb)],
        (first, first_other, table),
        "vvv",
        "h",
        scratch=[pltpu.VMEM((8, 8, cut, bb), F32), dma((8,))],
        cost=(3 * nc * cut * bb, 4 * nc * cut * bb),
    )
    second, row_mine, plane, col = call(
        sum_second,
        [(rest + rb // 2, bb), (rb, ni), (1, k), (cb, nj)],
        (core_own, row_own, plane_sum, col_own, x_in, *second_in, core),
        "vvvvvvvvh",
    )
    second_other = lax.ppermute(second, "bz", pairs(nbz, 1))
    core, plane_sketch, row_sketch, col_sketch = call(
        write_second,
        [(nc, ab, bb), (1, k), (rb, ni), (cb, nj)],
        (second, second_other, table, row_mine, plane, col, core),
        "vvvvvvh",
        "hhhh",
        scratch=[pltpu.VMEM((8, 8, rest, bb), F32), dma((8,)), pltpu.VMEM((rb, ni), F32), dma((3,))],
        cost=(3 * nc * rest * bb, 4 * nc * rest * bb),
        input_output_aliases={6: 0},
    )
    return plane_sketch, row_sketch.T, col_sketch.T, core


def stepwise(slab, plane_test, row_test, col_test, core_planes, core_rows, core_cols):
    einsum = functools.partial(jnp.einsum, precision=lax.Precision.HIGHEST)
    by_col = einsum("pij,jr->pir", slab, col_test)
    plane_part = einsum("pir,ir->pr", by_col, row_test)
    row_part = einsum("pir,pr->ir", by_col, plane_test)
    by_row = einsum("pij,ir->pjr", slab, row_test)
    col_part = einsum("pjr,pr->jr", by_row, plane_test)
    plane_sketch = lax.psum(plane_part, ("bx", "by"))
    row_sketch = lax.psum_scatter(row_part, ("by", "bz"), scatter_dimension=1, tiled=True)
    col_sketch = lax.psum_scatter(col_part, ("bx", "bz"), scatter_dimension=1, tiled=True)
    shrunk = einsum("pij,bj->pib", slab, core_cols)
    reduced = lax.psum_scatter(shrunk, "by", scatter_dimension=2, tiled=True)
    partial_value = einsum("pib,ai->pab", reduced, core_rows)
    partial_value = lax.psum_scatter(partial_value, "bx", scatter_dimension=1, tiled=True)
    both = lax.all_gather(partial_value, "bz", axis=0, tiled=True)
    core_sketch = einsum("cp,pab->cab", core_planes, both)
    return plane_sketch, row_sketch, col_sketch, core_sketch


def solution(mesh):
    in_specs = (
        P(("groups", "bz"), "bx", "by"),
        P("bz", None),
        P("bx", None),
        P("by", None),
        P("bz", None),
        P(None, "bx"),
        P(None, "by"),
    )
    out_specs = (
        P(("groups", "bz"), None),
        P(("groups", "bx"), ("by", "bz")),
        P(("groups", "by"), ("bx", "bz")),
        P(("groups", "bz"), "bx", "by"),
    )
    bricks = tuple(mesh.shape[a] for a in ("bx", "by", "bz"))
    body = functools.partial(direct, mesh) if bricks == DIRECT else stepwise
    return jax.shard_map(body, mesh=mesh, in_specs=in_specs, out_specs=out_specs, check_vma=False)
```

```python
import functools

import jax
import jax.numpy as jnp
from jax import lax
from jax.experimental import pallas as pl
from jax.experimental.pallas import tpu as pltpu
from jax.sharding import PartitionSpec as P

F32 = jnp.float32
BF16 = jnp.bfloat16
VMEM_LIMIT = 40 << 20
DIRECT = (4, 2, 2)
FIRST = 5
LAST = 16
FIRST_ORDER = (2, 1, 3)
SECOND_ORDER = (1, 2, 3)


def split(x):
    hi = x.astype(BF16)
    return hi, (x - hi.astype(F32)).astype(BF16)


def dot(a, b, contract):
    dims = ((contract[:1], contract[1:]), ((), ()))
    return lax.dot_general(a, b, dims, preferred_element_type=F32)


def rows_dot(a, b):
    m, n = a[0].shape[0], b[0].shape[0]
    r = dot(jnp.concatenate(a), jnp.concatenate(b), (1, 1))
    return r[:m, :n] + (r[:m, n:] + r[m:, :n])


def call(kernel, outs, operands, spaces, out_spaces=None, scratch=(), cost=None, **kw):
    spec = {
        "v": pl.BlockSpec(memory_space=pltpu.VMEM),
        "h": pl.BlockSpec(memory_space=pltpu.HBM),
    }
    out_spaces = out_spaces or "v" * len(outs)
    operands = [
        pltpu.with_memory_space_constraint(o, pltpu.HBM) if s == "h" else o for o, s in zip(operands, spaces)
    ]
    return pl.pallas_call(
        kernel,
        out_shape=[s if hasattr(s, "dtype") else jax.ShapeDtypeStruct(s, F32) for s in outs],
        in_specs=[spec[s] for s in spaces],
        out_specs=[spec[s] for s in out_spaces],
        scratch_shapes=list(scratch),
        cost_estimate=cost and pl.CostEstimate(flops=cost[0], bytes_accessed=cost[1], transcendentals=0),
        compiler_params=pltpu.CompilerParams(vmem_limit_bytes=VMEM_LIMIT),
        **kw,
    )(*operands)


def pairs(n, k):
    return [(i, i ^ k) for i in range(n)]


def block(i, size):
    return pl.ds(pl.multiple_of(i * size, size), size)


def read(sources, buffers, sem):
    copies = [pltpu.make_async_copy(s, b, sem.at[i]) for i, (s, b) in enumerate(zip(sources, buffers))]
    for c in copies:
        c.start()
    return copies


def others_columns(slab, cols, send, s_buf, c_buf, sem):
    other = 1 - lax.axis_index("by")
    bb = send.shape[0]
    copies = read((slab.at[0], cols.at[block(other, bb)]), (s_buf, c_buf), sem)
    copies[0].wait()
    brick = split(s_buf[...])
    copies[1].wait()
    send[...] = rows_dot(split(c_buf[...]), brick)


def own_terms(slab, cols, col_test, row_test, plane_test, core_rows, planes, after, *refs):
    own, row_own, row_away, plane_own, col_own, col_away, left, table, *bufs, sem = refs
    y, z = lax.axis_index("by"), lax.axis_index("bz")
    s_buf, rt_buf, pt_buf, ct_buf, c_buf, cr_buf, p_buf = bufs
    bb, ni = own.shape
    copies = read((slab.at[0], row_test, plane_test, col_test, cols.at[block(y, bb)], core_rows, planes), bufs, sem)
    for c in copies[:3]:
        c.wait()
    brick = split(s_buf[...])
    both = jnp.concatenate(brick)
    k = rt_buf.shape[1]
    hi, lo = split((rt_buf[...] * pt_buf[...]).T)
    by_row = dot(jnp.concatenate([jnp.concatenate([hi, hi], axis=1), jnp.concatenate([lo, lo], axis=1)]), both, (1, 0))
    by_row = by_row[:k] + by_row[k:]
    cb = col_own.shape[0] // 4
    for d in range(4):
        at = 2 * d * cb
        low, high = by_row[at : at + cb], by_row[at + cb : at + 2 * cb]
        col_own[d * cb : (d + 1) * cb] = jnp.where(z == 0, low, high)
        col_away[d * cb : (d + 1) * cb] = jnp.where(z == 0, high, low)
    copies[3].wait()
    hi, lo = split(ct_buf[...])
    by_col = dot(both, hi, (1, 0))
    by_col = by_col[:ni] + (by_col[ni:] + dot(brick[0], lo, (1, 0)))
    plane = jnp.sum(by_col * rt_buf[...], axis=0, keepdims=True)
    rows8 = lax.broadcasted_iota(jnp.int32, plane_own.shape, 0)
    plane_own[...] = jnp.where(rows8 == 0, plane[:, :ni], plane[:, ni:])
    turned = (by_col * pt_buf[...]).T
    rows = row_own.shape[0]
    low, high = turned[:rows], turned[rows:]
    row_own[...] = jnp.where(y == 0, low, high)
    row_away[...] = jnp.where(y == 0, high, low)
    copies[4].wait()
    own[...] = rows_dot(split(c_buf[...]), brick)
    copies[5].wait()
    hi, lo = split(cr_buf[...])
    left[:, :ni] = hi
    left[:, ni : 2 * ni] = lo
    left[:, 2 * ni :] = hi
    copies[6].wait()
    for i, p in enumerate((z, 1 - z)):
        table[i] = jnp.broadcast_to(p_buf[pl.ds(p, 1), :], table.shape[:0:-1]).T


def core_first(left, own, received, plane, right, *outs):
    x = lax.axis_index("bx")
    ni = own.shape[1]
    hi, lo = split(own[...] + received[...])
    right[:, :ni] = hi
    right[:, ni : 2 * ni] = hi
    right[:, 2 * ni :] = lo
    ab = left.shape[0] // 4
    for k, out in zip(FIRST_ORDER, outs):
        cut = (out.shape[0] - 8) // 2
        rows = pl.ds(pl.multiple_of((x ^ k) * ab, ab), cut)
        terms = dot(left[rows], right[...], (1, 1))
        out[:cut] = terms[:, :ni]
        out[cut : 2 * cut] = terms[:, ni:]
        out[2 * cut :] = plane[...]


def core_second(cut, left, right, col_terms, col_received, *refs):
    core_own, col_own, *outs = refs
    x = lax.axis_index("bx")
    ab = left.shape[0] // 4
    rest = ab - cut
    cb, wide = col_own.shape[0], core_own.shape[1]
    for k, out in zip(SECOND_ORDER, outs):
        rows = pl.ds(pl.multiple_of((x ^ k) * ab + cut, 16), rest)
        out[:rest] = dot(left[rows], right[...], (1, 1))
        col = col_terms[block(x ^ k, cb)] + col_received[block(x ^ k, cb)]
        for part in range(col.shape[1] // wide):
            out[rest + part * cb : rest + (part + 1) * cb] = col[:, part * wide : (part + 1) * wide]
    col_own[...] = col_terms[block(x, cb)] + col_received[block(x, cb)]
    core_own[...] = dot(left[block(x, ab)], right[...], (1, 1))


def sum_first(core_own, row_away, plane_own, in_a, in_b, in_c, out, x_send, plane_sum):
    cut, rows = out.shape[0], row_away.shape[0]
    ni = row_away.shape[1]
    for part in range(2):
        lanes = slice(part * ni, (part + 1) * ni)
        got = slice(part * cut, (part + 1) * cut)
        out[:, lanes] = (core_own[:cut, lanes] + in_a[got]) + (in_b[got] + in_c[got])
    plane = (plane_own[...] + in_a[2 * cut :]) + (in_b[2 * cut :] + in_c[2 * cut :])
    plane_sum[...] = plane
    x_send[:rows] = row_away[...]
    x_send[rows:] = plane


def sum_second(core_own, row_own, plane_sum, col_own, x_received, in_a, in_b, in_c, token, out, row_mine, plane, col):
    z = lax.axis_index("bz")
    rows, ni = row_own.shape
    rb, cb = rows // 2, col_own.shape[0]
    rest = in_a.shape[0] - col_own.shape[1] // out.shape[1] * cb
    out[:rest] = (core_own[core_own.shape[0] - rest :] + in_a[:rest]) + (in_b[:rest] + in_c[:rest])
    mine, away = block(z, rb), block(1 - z, rb)
    row_mine[...] = row_own[mine] + x_received[mine]
    turned = row_own[away] + x_received[away]
    out[rest:, :ni] = turned[: rb // 2]
    out[rest:, ni:] = turned[rb // 2 :]
    total = plane_sum[...] + x_received[rows:]
    for part in range(plane.shape[1] // ni):
        plane[:, part * ni : (part + 1) * ni] = total[part : part + 1]
    wide = out.shape[1]
    for part in range(col.shape[1] // wide):
        lanes = slice(part * wide, (part + 1) * wide)
        got = slice(rest + part * cb, rest + (part + 1) * cb)
        col[:, lanes] = (col_own[:, lanes] + in_a[got]) + (in_b[got] + in_c[got])


def write(at, planes, own, other, table, out, buf, sem):
    nb, cb, rows = buf.shape[:3]
    start, steps = planes[0] // cb, (planes[1] - planes[0]) // cb
    nb = min(nb, steps)

    def copy(s, slot):
        return pltpu.make_async_copy(buf.at[slot], out.at[block(start + s, cb), pl.ds(at, rows)], sem.at[slot])

    def step(s, _):
        slot = lax.rem(s, nb)

        @pl.when(s >= nb)
        def _():
            copy(s - nb, slot).wait()

        for c in range(cb):
            row = pl.ds((start + s) * cb + c, 1)
            buf[slot, c] = table[0, row] * own[:rows] + table[1, row] * other[:rows]
        copy(s, slot).start()
        return 0

    lax.fori_loop(0, steps, step, 0)

    def drain(s, _):
        copy(s, lax.rem(s, nb)).wait()
        return 0

    lax.fori_loop(steps - nb, steps, drain, 0)


def write_first(own, other, table, out, token, buf, sem):
    write(0, (0, out.shape[0] - LAST), own, other, table, out, buf, sem)
    token[...] = jnp.zeros_like(token)


def write_rest(own, other, table, core, out, buf, sem):
    write(0, (out.shape[0] - LAST, out.shape[0]), own, other, table, out, buf, sem)


def write_second(own, other, table, row_mine, plane, col, core, out, plane_out, row_out, col_out, buf, sem, row_buf, out_sem):
    rest, ni = buf.shape[2], row_buf.shape[1]
    half = row_buf.shape[0] // 2
    row_buf[:half] = row_mine[:half] + other[rest:, :ni]
    row_buf[half:] = row_mine[half:] + other[rest:, ni:]
    copies = read((plane, row_buf, col), (plane_out, row_out, col_out), out_sem)
    write(out.shape[1] - rest, (0, out.shape[0]), own, other, table, out, buf, sem)
    for c in copies:
        c.wait()


def direct(mesh, slab, plane_test, row_test, col_test, core_planes, core_rows, core_cols):
    nbx, nby, nbz = DIRECT
    _, ni, nj = slab.shape
    k = row_test.shape[1]
    na, nc = core_rows.shape[0], core_planes.shape[0]
    ab, bb = na // nbx, core_cols.shape[0] // nby
    rb, cb = k // (nby * nbz), k // (nbx * nbz)
    cut = FIRST * ab // 8
    rest = ab - cut
    dma = pltpu.SemaphoreType.DMA

    (x_send,) = call(
        others_columns,
        [(bb, ni)],
        (slab, core_cols),
        "hh",
        scratch=[pltpu.VMEM((ni, nj), F32), pltpu.VMEM((bb, nj), F32), dma((2,))],
        cost=(6 * ni * nj * bb, 4 * (ni + bb) * nj),
    )
    x_in = lax.ppermute(x_send, "by", pairs(nby, 1))

    own, row_own, row_away, plane_own, col_terms, col_away, left, table = call(
        own_terms,
        [
            (bb, ni),
            (nbz * rb, ni),
            (nbz * rb, ni),
            (8, ni),
            (nbx * cb, nj),
            (nbx * cb, nj),
            jax.ShapeDtypeStruct((na, 3 * ni), BF16),
            (2, nc, bb),
        ],
        (slab, core_cols, col_test, row_test, plane_test, core_rows, core_planes.T, x_send),
        "hhhhhhhv",
        scratch=[
            pltpu.VMEM((ni, nj), F32),
            pltpu.VMEM((ni, k), F32),
            pltpu.VMEM((1, k), F32),
            pltpu.VMEM((nj, k), F32),
            pltpu.VMEM((bb, nj), F32),
            pltpu.VMEM((na, ni), F32),
            pltpu.VMEM((nbz, nc), F32),
            dma((7,)),
        ],
        cost=(6 * ni * nj * (bb + 2 * k), 4 * (ni * nj + bb * nj + nj * k)),
    )
    right, *sends = call(
        core_first,
        [jax.ShapeDtypeStruct((bb, 3 * ni), BF16)] + [(2 * cut + 8, ni)] * 3,
        (left, own, x_in, plane_own),
        "vvvv",
        cost=(6 * ni * bb * 3 * cut, 4 * ni * bb),
    )
    col_away, *sends = lax.optimization_barrier((col_away, *sends))
    first_in = [lax.ppermute(s, "bx", pairs(nbx, i)) for i, s in zip(FIRST_ORDER, sends)]
    col_in = lax.ppermute(col_away, "bz", pairs(nbz, 1))

    core_own, col_own, *sends = call(
        functools.partial(core_second, cut),
        [(ab, bb), (cb, nj)] + [(rest + cb * nj // bb, bb)] * 3,
        (left, right, col_terms, col_in),
        "vvvv",
        cost=(6 * ni * bb * 4 * ab, 4 * ni * bb),
    )
    second_in = [lax.ppermute(s, "bx", pairs(nbx, i)) for i, s in zip(SECOND_ORDER, sends)]

    first, x_send, plane_sum = call(
        sum_first,
        [(cut, bb), (nbz * rb + 8, ni), (8, ni)],
        (core_own, row_away, plane_own, *first_in),
        "vvvvvv",
    )
    first_other = lax.ppermute(first, "bz", pairs(nbz, 1))
    x_in = lax.ppermute(x_send, "by", pairs(nby, 1))
    early = nc - LAST
    core, token = call(
        write_first,
        [(nc, ab, bb), (8, ni)],
        (first, first_other, table),
        "vvv",
        "hv",
        scratch=[pltpu.VMEM((16, 4, cut, bb), F32), dma((16,))],
        cost=(3 * early * cut * bb, 4 * early * cut * bb),
    )
    second, row_mine, plane, col = call(
        sum_second,
        [(rest + rb // 2, bb), (rb, ni), (1, k), (cb, nj)],
        (core_own, row_own, plane_sum, col_own, x_in, *second_in, token),
        "v" * 9,
    )
    second_other = lax.ppermute(second, "bz", pairs(nbz, 1))
    (core,) = call(
        write_rest,
        [(nc, ab, bb)],
        (first, first_other, table, core),
        "vvvh",
        "h",
        scratch=[pltpu.VMEM((16, 4, cut, bb), F32), dma((16,))],
        cost=(3 * LAST * cut * bb, 4 * LAST * cut * bb),
        input_output_aliases={3: 0},
    )
    core, plane_sketch, row_sketch, col_sketch = call(
        write_second,
        [(nc, ab, bb), (1, k), (rb, ni), (cb, nj)],
        (second, second_other, table, row_mine, plane, col, core),
        "vvvvvvh",
        "hhhh",
        scratch=[pltpu.VMEM((8, 8, rest, bb), F32), dma((8,)), pltpu.VMEM((rb, ni), F32), dma((3,))],
        cost=(3 * nc * rest * bb, 4 * nc * rest * bb),
        input_output_aliases={6: 0},
    )
    return plane_sketch, row_sketch.T, col_sketch.T, core


def stepwise(slab, plane_test, row_test, col_test, core_planes, core_rows, core_cols):
    einsum = functools.partial(jnp.einsum, precision=lax.Precision.HIGHEST)
    by_col = einsum("pij,jr->pir", slab, col_test)
    plane_part = einsum("pir,ir->pr", by_col, row_test)
    row_part = einsum("pir,pr->ir", by_col, plane_test)
    by_row = einsum("pij,ir->pjr", slab, row_test)
    col_part = einsum("pjr,pr->jr", by_row, plane_test)
    plane_sketch = lax.psum(plane_part, ("bx", "by"))
    row_sketch = lax.psum_scatter(row_part, ("by", "bz"), scatter_dimension=1, tiled=True)
    col_sketch = lax.psum_scatter(col_part, ("bx", "bz"), scatter_dimension=1, tiled=True)
    shrunk = einsum("pij,bj->pib", slab, core_cols)
    reduced = lax.psum_scatter(shrunk, "by", scatter_dimension=2, tiled=True)
    partial_value = einsum("pib,ai->pab", reduced, core_rows)
    partial_value = lax.psum_scatter(partial_value, "bx", scatter_dimension=1, tiled=True)
    both = lax.all_gather(partial_value, "bz", axis=0, tiled=True)
    core_sketch = einsum("cp,pab->cab", core_planes, both)
    return plane_sketch, row_sketch, col_sketch, core_sketch


def solution(mesh):
    in_specs = (
        P(("groups", "bz"), "bx", "by"),
        P("bz", None),
        P("bx", None),
        P("by", None),
        P("bz", None),
        P(None, "bx"),
        P(None, "by"),
    )
    out_specs = (
        P(("groups", "bz"), None),
        P(("groups", "bx"), ("by", "bz")),
        P(("groups", "by"), ("bx", "bz")),
        P(("groups", "bz"), "bx", "by"),
    )
    bricks = tuple(mesh.shape[a] for a in ("bx", "by", "bz"))
    body = functools.partial(direct, mesh) if bricks == DIRECT else stepwise
    return jax.shard_map(body, mesh=mesh, in_specs=in_specs, out_specs=out_specs, check_vma=False)
```

```python
import functools

import jax
import jax.numpy as jnp
from jax import lax
from jax.experimental import pallas as pl
from jax.experimental.pallas import tpu as pltpu
from jax.sharding import PartitionSpec as P

F32 = jnp.float32
BF16 = jnp.bfloat16
VMEM_LIMIT = 40 << 20
DIRECT = (4, 2, 2)
FIRST = 5
LAST = 16
FIRST_ORDER = (2, 1, 3)
SECOND_ORDER = (1, 2, 3)


def split(x):
    hi = x.astype(BF16)
    return hi, (x - hi.astype(F32)).astype(BF16)


def dot(a, b, contract):
    dims = ((contract[:1], contract[1:]), ((), ()))
    return lax.dot_general(a, b, dims, preferred_element_type=F32)


def rows_dot(a, b):
    m, n = a[0].shape[0], b[0].shape[0]
    r = dot(jnp.concatenate(a), jnp.concatenate(b), (1, 1))
    return r[:m, :n] + (r[:m, n:] + r[m:, :n])


def call(kernel, outs, operands, spaces, out_spaces=None, scratch=(), cost=None, **kw):
    spec = {
        "v": pl.BlockSpec(memory_space=pltpu.VMEM),
        "h": pl.BlockSpec(memory_space=pltpu.HBM),
    }
    out_spaces = out_spaces or "v" * len(outs)
    operands = [
        pltpu.with_memory_space_constraint(o, pltpu.HBM) if s == "h" else o for o, s in zip(operands, spaces)
    ]
    return pl.pallas_call(
        kernel,
        out_shape=[s if hasattr(s, "dtype") else jax.ShapeDtypeStruct(s, F32) for s in outs],
        in_specs=[spec[s] for s in spaces],
        out_specs=[spec[s] for s in out_spaces],
        scratch_shapes=list(scratch),
        cost_estimate=cost and pl.CostEstimate(flops=cost[0], bytes_accessed=cost[1], transcendentals=0),
        compiler_params=pltpu.CompilerParams(vmem_limit_bytes=VMEM_LIMIT),
        **kw,
    )(*operands)


def pairs(n, k):
    return [(i, i ^ k) for i in range(n)]


def block(i, size):
    return pl.ds(pl.multiple_of(i * size, size), size)


def read(sources, buffers, sem):
    copies = [pltpu.make_async_copy(s, b, sem.at[i]) for i, (s, b) in enumerate(zip(sources, buffers))]
    for c in copies:
        c.start()
    return copies


def others_columns(slab, cols, send, s_buf, c_buf, sem):
    other = 1 - lax.axis_index("by")
    bb = send.shape[0]
    copies = read((slab.at[0], cols.at[block(other, bb)]), (s_buf, c_buf), sem)
    copies[0].wait()
    brick = split(s_buf[...])
    copies[1].wait()
    send[...] = rows_dot(split(c_buf[...]), brick)


def own_terms(slab, cols, col_test, row_test, plane_test, core_rows, planes, after, *refs):
    own, row_own, row_away, plane_own, col_own, col_away, left, table, *bufs, sem = refs
    y, z = lax.axis_index("by"), lax.axis_index("bz")
    s_buf, rt_buf, pt_buf, ct_buf, c_buf, cr_buf, p_buf = bufs
    bb, ni = own.shape
    copies = read((slab.at[0], row_test, plane_test, col_test, cols.at[block(y, bb)], core_rows, planes), bufs, sem)
    for c in copies[:3]:
        c.wait()
    brick = split(s_buf[...])
    both = jnp.concatenate(brick)
    k = rt_buf.shape[1]
    hi, lo = split((rt_buf[...] * pt_buf[...]).T)
    by_row = dot(jnp.concatenate([jnp.concatenate([hi, hi], axis=1), jnp.concatenate([lo, lo], axis=1)]), both, (1, 0))
    by_row = by_row[:k] + by_row[k:]
    cb = col_own.shape[0] // 4
    for d in range(4):
        at = 2 * d * cb
        low, high = by_row[at : at + cb], by_row[at + cb : at + 2 * cb]
        col_own[d * cb : (d + 1) * cb] = jnp.where(z == 0, low, high)
        col_away[d * cb : (d + 1) * cb] = jnp.where(z == 0, high, low)
    copies[3].wait()
    hi, lo = split(ct_buf[...])
    by_col = dot(both, hi, (1, 0))
    by_col = by_col[:ni] + (by_col[ni:] + dot(brick[0], lo, (1, 0)))
    plane = jnp.sum(by_col * rt_buf[...], axis=0, keepdims=True)
    rows8 = lax.broadcasted_iota(jnp.int32, plane_own.shape, 0)
    plane_own[...] = jnp.where(rows8 == 0, plane[:, :ni], plane[:, ni:])
    turned = (by_col * pt_buf[...]).T
    rows = row_own.shape[0]
    low, high = turned[:rows], turned[rows:]
    row_own[...] = jnp.where(y == 0, low, high)
    row_away[...] = jnp.where(y == 0, high, low)
    copies[4].wait()
    own[...] = rows_dot(split(c_buf[...]), brick)
    copies[5].wait()
    hi, lo = split(cr_buf[...])
    left[:, :ni] = hi
    left[:, ni : 2 * ni] = lo
    left[:, 2 * ni :] = hi
    copies[6].wait()
    for i, p in enumerate((z, 1 - z)):
        table[i] = jnp.broadcast_to(p_buf[pl.ds(p, 1), :], table.shape[:0:-1]).T


def core_first(left, own, received, plane, right, *outs):
    x = lax.axis_index("bx")
    ni = own.shape[1]
    hi, lo = split(own[...] + received[...])
    right[:, :ni] = hi
    right[:, ni : 2 * ni] = hi
    right[:, 2 * ni :] = lo
    ab = left.shape[0] // 4
    cut = (outs[0].shape[0] - 8) // 2
    rows = [left[pl.ds(pl.multiple_of((x ^ k) * ab, ab), cut)] for k in FIRST_ORDER]
    stacked = dot(jnp.concatenate(rows), right[...], (1, 1))
    for i, out in enumerate(outs):
        terms = stacked[i * cut : (i + 1) * cut]
        out[:cut] = terms[:, :ni]
        out[cut : 2 * cut] = terms[:, ni:]
        out[2 * cut :] = plane[...]


def core_second(cut, left, right, col_terms, col_received, *refs):
    core_own, col_own, *outs = refs
    x = lax.axis_index("bx")
    ab = left.shape[0] // 4
    rest = ab - cut
    cb, wide = col_own.shape[0], core_own.shape[1]
    rows = [left[pl.ds(pl.multiple_of((x ^ k) * ab + cut, 16), rest)] for k in SECOND_ORDER]
    stacked = dot(jnp.concatenate([*rows, left[block(x, ab)]]), right[...], (1, 1))
    core_own[...] = stacked[3 * rest :]
    for i, (k, out) in enumerate(zip(SECOND_ORDER, outs)):
        out[:rest] = stacked[i * rest : (i + 1) * rest]
        col = col_terms[block(x ^ k, cb)] + col_received[block(x ^ k, cb)]
        for part in range(col.shape[1] // wide):
            out[rest + part * cb : rest + (part + 1) * cb] = col[:, part * wide : (part + 1) * wide]
    col_own[...] = col_terms[block(x, cb)] + col_received[block(x, cb)]


def sum_first(core_own, row_away, plane_own, in_a, in_b, in_c, out, x_send, plane_sum):
    cut, rows = out.shape[0], row_away.shape[0]
    ni = row_away.shape[1]
    for part in range(2):
        lanes = slice(part * ni, (part + 1) * ni)
        got = slice(part * cut, (part + 1) * cut)
        out[:, lanes] = (core_own[:cut, lanes] + in_a[got]) + (in_b[got] + in_c[got])
    plane = (plane_own[...] + in_a[2 * cut :]) + (in_b[2 * cut :] + in_c[2 * cut :])
    plane_sum[...] = plane
    x_send[:rows] = row_away[...]
    x_send[rows:] = plane


def sum_second(core_own, row_own, plane_sum, col_own, x_received, in_a, in_b, in_c, token, out, row_mine, plane, col):
    z = lax.axis_index("bz")
    rows, ni = row_own.shape
    rb, cb = rows // 2, col_own.shape[0]
    rest = in_a.shape[0] - col_own.shape[1] // out.shape[1] * cb
    out[:rest] = (core_own[core_own.shape[0] - rest :] + in_a[:rest]) + (in_b[:rest] + in_c[:rest])
    mine, away = block(z, rb), block(1 - z, rb)
    row_mine[...] = row_own[mine] + x_received[mine]
    turned = row_own[away] + x_received[away]
    out[rest:, :ni] = turned[: rb // 2]
    out[rest:, ni:] = turned[rb // 2 :]
    total = plane_sum[...] + x_received[rows:]
    for part in range(plane.shape[1] // ni):
        plane[:, part * ni : (part + 1) * ni] = total[part : part + 1]
    wide = out.shape[1]
    for part in range(col.shape[1] // wide):
        lanes = slice(part * wide, (part + 1) * wide)
        got = slice(rest + part * cb, rest + (part + 1) * cb)
        col[:, lanes] = (col_own[:, lanes] + in_a[got]) + (in_b[got] + in_c[got])


def write(at, planes, own, other, table, out, buf, sem):
    nb, cb, rows = buf.shape[:3]
    start, steps = planes[0] // cb, (planes[1] - planes[0]) // cb
    nb = min(nb, steps)

    def copy(s, slot):
        return pltpu.make_async_copy(buf.at[slot], out.at[block(start + s, cb), pl.ds(at, rows)], sem.at[slot])

    def step(s, _):
        slot = lax.rem(s, nb)

        @pl.when(s >= nb)
        def _():
            copy(s - nb, slot).wait()

        for c in range(cb):
            row = pl.ds((start + s) * cb + c, 1)
            buf[slot, c] = table[0, row] * own[:rows] + table[1, row] * other[:rows]
        copy(s, slot).start()
        return 0

    lax.fori_loop(0, steps, step, 0)

    def drain(s, _):
        copy(s, lax.rem(s, nb)).wait()
        return 0

    lax.fori_loop(steps - nb, steps, drain, 0)


def write_first(own, other, table, out, token, buf, sem):
    write(0, (0, out.shape[0] - LAST), own, other, table, out, buf, sem)
    token[...] = jnp.zeros_like(token)


def write_rest(own, other, table, core, out, buf, sem):
    write(0, (out.shape[0] - LAST, out.shape[0]), own, other, table, out, buf, sem)


def write_second(own, other, table, row_mine, plane, col, core, out, plane_out, row_out, col_out, buf, sem, row_buf, out_sem):
    rest, ni = buf.shape[2], row_buf.shape[1]
    half = row_buf.shape[0] // 2
    row_buf[:half] = row_mine[:half] + other[rest:, :ni]
    row_buf[half:] = row_mine[half:] + other[rest:, ni:]
    copies = read((plane, row_buf, col), (plane_out, row_out, col_out), out_sem)
    write(out.shape[1] - rest, (0, out.shape[0]), own, other, table, out, buf, sem)
    for c in copies:
        c.wait()


def direct(mesh, slab, plane_test, row_test, col_test, core_planes, core_rows, core_cols):
    nbx, nby, nbz = DIRECT
    _, ni, nj = slab.shape
    k = row_test.shape[1]
    na, nc = core_rows.shape[0], core_planes.shape[0]
    ab, bb = na // nbx, core_cols.shape[0] // nby
    rb, cb = k // (nby * nbz), k // (nbx * nbz)
    cut = FIRST * ab // 8
    rest = ab - cut
    dma = pltpu.SemaphoreType.DMA

    (x_send,) = call(
        others_columns,
        [(bb, ni)],
        (slab, core_cols),
        "hh",
        scratch=[pltpu.VMEM((ni, nj), F32), pltpu.VMEM((bb, nj), F32), dma((2,))],
        cost=(6 * ni * nj * bb, 4 * (ni + bb) * nj),
    )
    x_in = lax.ppermute(x_send, "by", pairs(nby, 1))

    own, row_own, row_away, plane_own, col_terms, col_away, left, table = call(
        own_terms,
        [
            (bb, ni),
            (nbz * rb, ni),
            (nbz * rb, ni),
            (8, ni),
            (nbx * cb, nj),
            (nbx * cb, nj),
            jax.ShapeDtypeStruct((na, 3 * ni), BF16),
            (2, nc, bb),
        ],
        (slab, core_cols, col_test, row_test, plane_test, core_rows, core_planes.T, x_send),
        "hhhhhhhv",
        scratch=[
            pltpu.VMEM((ni, nj), F32),
            pltpu.VMEM((ni, k), F32),
            pltpu.VMEM((1, k), F32),
            pltpu.VMEM((nj, k), F32),
            pltpu.VMEM((bb, nj), F32),
            pltpu.VMEM((na, ni), F32),
            pltpu.VMEM((nbz, nc), F32),
            dma((7,)),
        ],
        cost=(6 * ni * nj * (bb + 2 * k), 4 * (ni * nj + bb * nj + nj * k)),
    )
    right, *sends = call(
        core_first,
        [jax.ShapeDtypeStruct((bb, 3 * ni), BF16)] + [(2 * cut + 8, ni)] * 3,
        (left, own, x_in, plane_own),
        "vvvv",
        cost=(6 * ni * bb * 3 * cut, 4 * ni * bb),
    )
    col_away, *sends = lax.optimization_barrier((col_away, *sends))
    first_in = [lax.ppermute(s, "bx", pairs(nbx, i)) for i, s in zip(FIRST_ORDER, sends)]
    col_in = lax.ppermute(col_away, "bz", pairs(nbz, 1))

    core_own, col_own, *sends = call(
        functools.partial(core_second, cut),
        [(ab, bb), (cb, nj)] + [(rest + cb * nj // bb, bb)] * 3,
        (left, right, col_terms, col_in),
        "vvvv",
        cost=(6 * ni * bb * 4 * ab, 4 * ni * bb),
    )
    second_in = [lax.ppermute(s, "bx", pairs(nbx, i)) for i, s in zip(SECOND_ORDER, sends)]

    first, x_send, plane_sum = call(
        sum_first,
        [(cut, bb), (nbz * rb + 8, ni), (8, ni)],
        (core_own, row_away, plane_own, *first_in),
        "vvvvvv",
    )
    first_other = lax.ppermute(first, "bz", pairs(nbz, 1))
    x_in = lax.ppermute(x_send, "by", pairs(nby, 1))
    early = nc - LAST
    core, token = call(
        write_first,
        [(nc, ab, bb), (8, ni)],
        (first, first_other, table),
        "vvv",
        "hv",
        scratch=[pltpu.VMEM((16, 4, cut, bb), F32), dma((16,))],
        cost=(3 * early * cut * bb, 4 * early * cut * bb),
    )
    second, row_mine, plane, col = call(
        sum_second,
        [(rest + rb // 2, bb), (rb, ni), (1, k), (cb, nj)],
        (core_own, row_own, plane_sum, col_own, x_in, *second_in, token),
        "v" * 9,
    )
    second_other = lax.ppermute(second, "bz", pairs(nbz, 1))
    (core,) = call(
        write_rest,
        [(nc, ab, bb)],
        (first, first_other, table, core),
        "vvvh",
        "h",
        scratch=[pltpu.VMEM((16, 4, cut, bb), F32), dma((16,))],
        cost=(3 * LAST * cut * bb, 4 * LAST * cut * bb),
        input_output_aliases={3: 0},
    )
    core, plane_sketch, row_sketch, col_sketch = call(
        write_second,
        [(nc, ab, bb), (1, k), (rb, ni), (cb, nj)],
        (second, second_other, table, row_mine, plane, col, core),
        "vvvvvvh",
        "hhhh",
        scratch=[pltpu.VMEM((8, 8, rest, bb), F32), dma((8,)), pltpu.VMEM((rb, ni), F32), dma((3,))],
        cost=(3 * nc * rest * bb, 4 * nc * rest * bb),
        input_output_aliases={6: 0},
    )
    return plane_sketch, row_sketch.T, col_sketch.T, core


def stepwise(slab, plane_test, row_test, col_test, core_planes, core_rows, core_cols):
    einsum = functools.partial(jnp.einsum, precision=lax.Precision.HIGHEST)
    by_col = einsum("pij,jr->pir", slab, col_test)
    plane_part = einsum("pir,ir->pr", by_col, row_test)
    row_part = einsum("pir,pr->ir", by_col, plane_test)
    by_row = einsum("pij,ir->pjr", slab, row_test)
    col_part = einsum("pjr,pr->jr", by_row, plane_test)
    plane_sketch = lax.psum(plane_part, ("bx", "by"))
    row_sketch = lax.psum_scatter(row_part, ("by", "bz"), scatter_dimension=1, tiled=True)
    col_sketch = lax.psum_scatter(col_part, ("bx", "bz"), scatter_dimension=1, tiled=True)
    shrunk = einsum("pij,bj->pib", slab, core_cols)
    reduced = lax.psum_scatter(shrunk, "by", scatter_dimension=2, tiled=True)
    partial_value = einsum("pib,ai->pab", reduced, core_rows)
    partial_value = lax.psum_scatter(partial_value, "bx", scatter_dimension=1, tiled=True)
    both = lax.all_gather(partial_value, "bz", axis=0, tiled=True)
    core_sketch = einsum("cp,pab->cab", core_planes, both)
    return plane_sketch, row_sketch, col_sketch, core_sketch


def solution(mesh):
    in_specs = (
        P(("groups", "bz"), "bx", "by"),
        P("bz", None),
        P("bx", None),
        P("by", None),
        P("bz", None),
        P(None, "bx"),
        P(None, "by"),
    )
    out_specs = (
        P(("groups", "bz"), None),
        P(("groups", "bx"), ("by", "bz")),
        P(("groups", "by"), ("bx", "bz")),
        P(("groups", "bz"), "bx", "by"),
    )
    bricks = tuple(mesh.shape[a] for a in ("bx", "by", "bz"))
    body = functools.partial(direct, mesh) if bricks == DIRECT else stepwise
    return jax.shard_map(body, mesh=mesh, in_specs=in_specs, out_specs=out_specs, check_vma=False)
```

```python
import functools

import jax
import jax.numpy as jnp
from jax import lax
from jax.experimental import pallas as pl
from jax.experimental.pallas import tpu as pltpu
from jax.sharding import PartitionSpec as P

F32 = jnp.float32
BF16 = jnp.bfloat16
VMEM_LIMIT = 40 << 20
DIRECT = (4, 2, 2)
FIRST = 5
LAST = 16
FIRST_ORDER = (2, 1, 3)
SECOND_ORDER = (1, 2, 3)


def split(x):
    hi = x.astype(BF16)
    return hi, (x - hi.astype(F32)).astype(BF16)


def dot(a, b, contract):
    dims = ((contract[:1], contract[1:]), ((), ()))
    return lax.dot_general(a, b, dims, preferred_element_type=F32)


def rows_dot(a, b):
    m, n = a[0].shape[0], b[0].shape[0]
    r = dot(jnp.concatenate(a), jnp.concatenate(b), (1, 1))
    return r[:m, :n] + (r[:m, n:] + r[m:, :n])


def call(kernel, outs, operands, spaces, out_spaces=None, scratch=(), cost=None, **kw):
    spec = {
        "v": pl.BlockSpec(memory_space=pltpu.VMEM),
        "h": pl.BlockSpec(memory_space=pltpu.HBM),
    }
    out_spaces = out_spaces or "v" * len(outs)
    operands = [
        pltpu.with_memory_space_constraint(o, pltpu.HBM) if s == "h" else o for o, s in zip(operands, spaces)
    ]
    return pl.pallas_call(
        kernel,
        out_shape=[s if hasattr(s, "dtype") else jax.ShapeDtypeStruct(s, F32) for s in outs],
        in_specs=[spec[s] for s in spaces],
        out_specs=[spec[s] for s in out_spaces],
        scratch_shapes=list(scratch),
        cost_estimate=cost and pl.CostEstimate(flops=cost[0], bytes_accessed=cost[1], transcendentals=0),
        compiler_params=pltpu.CompilerParams(vmem_limit_bytes=VMEM_LIMIT),
        **kw,
    )(*operands)


def pairs(n, k):
    return [(i, i ^ k) for i in range(n)]


def block(i, size):
    return pl.ds(pl.multiple_of(i * size, size), size)


def read(sources, buffers, sem):
    copies = [pltpu.make_async_copy(s, b, sem.at[i]) for i, (s, b) in enumerate(zip(sources, buffers))]
    for c in copies:
        c.start()
    return copies


def others_columns(slab, cols, send, s_buf, c_buf, sem):
    other = 1 - lax.axis_index("by")
    bb = send.shape[0]
    copies = read((slab.at[0], cols.at[block(other, bb)]), (s_buf, c_buf), sem)
    copies[0].wait()
    brick = split(s_buf[...])
    copies[1].wait()
    send[...] = rows_dot(split(c_buf[...]), brick)


def own_terms(slab, cols, col_test, row_test, plane_test, core_rows, planes, after, *refs):
    own, row_own, row_away, plane_own, col_own, col_away, left, table, *bufs, sem = refs
    y, z = lax.axis_index("by"), lax.axis_index("bz")
    s_buf, rt_buf, pt_buf, ct_buf, c_buf, cr_buf, p_buf = bufs
    bb, ni = own.shape
    copies = read((slab.at[0], row_test, plane_test, col_test, cols.at[block(y, bb)], core_rows, planes), bufs, sem)
    for c in copies[:3]:
        c.wait()
    brick = split(s_buf[...])
    both = jnp.concatenate(brick)
    k = rt_buf.shape[1]
    hi, lo = split((rt_buf[...] * pt_buf[...]).T)
    by_row = dot(jnp.concatenate([jnp.concatenate([hi, hi], axis=1), jnp.concatenate([lo, lo], axis=1)]), both, (1, 0))
    by_row = by_row[:k] + by_row[k:]
    cb = col_own.shape[0] // 4
    for d in range(4):
        at = 2 * d * cb
        low, high = by_row[at : at + cb], by_row[at + cb : at + 2 * cb]
        col_own[d * cb : (d + 1) * cb] = jnp.where(z == 0, low, high)
        col_away[d * cb : (d + 1) * cb] = jnp.where(z == 0, high, low)
    copies[3].wait()
    hi, lo = split(ct_buf[...])
    by_col = dot(both, hi, (1, 0))
    by_col = by_col[:ni] + (by_col[ni:] + dot(brick[0], lo, (1, 0)))
    plane = jnp.sum(by_col * rt_buf[...], axis=0, keepdims=True)
    rows8 = lax.broadcasted_iota(jnp.int32, plane_own.shape, 0)
    plane_own[...] = jnp.where(rows8 == 0, plane[:, :ni], plane[:, ni:])
    turned = (by_col * pt_buf[...]).T
    rows = row_own.shape[0]
    low, high = turned[:rows], turned[rows:]
    row_own[...] = jnp.where(y == 0, low, high)
    row_away[...] = jnp.where(y == 0, high, low)
    copies[4].wait()
    own[...] = rows_dot(split(c_buf[...]), brick)
    copies[5].wait()
    hi, lo = split(cr_buf[...])
    left[:, :ni] = hi
    left[:, ni : 2 * ni] = lo
    left[:, 2 * ni :] = hi
    copies[6].wait()
    for i, p in enumerate((z, 1 - z)):
        table[i] = jnp.broadcast_to(p_buf[pl.ds(p, 1), :], table.shape[:0:-1]).T


def core_first(left, own, received, plane, right, *outs):
    x = lax.axis_index("bx")
    ni = own.shape[1]
    hi, lo = split(own[...] + received[...])
    right[:, :ni] = hi
    right[:, ni : 2 * ni] = hi
    right[:, 2 * ni :] = lo
    ab = left.shape[0] // 4
    cut = (outs[0].shape[0] - 8) // 2
    rows = [left[pl.ds(pl.multiple_of((x ^ k) * ab, ab), cut)] for k in FIRST_ORDER]
    stacked = dot(jnp.concatenate(rows), right[...], (1, 1))
    for i, out in enumerate(outs):
        terms = stacked[i * cut : (i + 1) * cut]
        out[:cut] = terms[:, :ni]
        out[cut : 2 * cut] = terms[:, ni:]
        out[2 * cut :] = plane[...]


def core_second(cut, left, right, col_terms, col_received, *refs):
    core_own, col_own, *outs = refs
    x = lax.axis_index("bx")
    ab = left.shape[0] // 4
    rest = ab - cut
    cb, wide = col_own.shape[0], core_own.shape[1]
    rows = [left[pl.ds(pl.multiple_of((x ^ k) * ab + cut, 16), rest)] for k in SECOND_ORDER]
    stacked = dot(jnp.concatenate([*rows, left[block(x, ab)]]), right[...], (1, 1))
    core_own[...] = stacked[3 * rest :]
    for i, (k, out) in enumerate(zip(SECOND_ORDER, outs)):
        out[:rest] = stacked[i * rest : (i + 1) * rest]
        col = col_terms[block(x ^ k, cb)] + col_received[block(x ^ k, cb)]
        for part in range(col.shape[1] // wide):
            out[rest + part * cb : rest + (part + 1) * cb] = col[:, part * wide : (part + 1) * wide]
    col_own[...] = col_terms[block(x, cb)] + col_received[block(x, cb)]


def sum_first(core_own, row_away, plane_own, in_a, in_b, in_c, out, x_send, plane_sum):
    cut, rows = out.shape[0], row_away.shape[0]
    ni = row_away.shape[1]
    for part in range(2):
        lanes = slice(part * ni, (part + 1) * ni)
        got = slice(part * cut, (part + 1) * cut)
        out[:, lanes] = (core_own[:cut, lanes] + in_a[got]) + (in_b[got] + in_c[got])
    plane = (plane_own[...] + in_a[2 * cut :]) + (in_b[2 * cut :] + in_c[2 * cut :])
    plane_sum[...] = plane
    x_send[:rows] = row_away[...]
    x_send[rows:] = plane


def sum_second(core_own, row_own, plane_sum, col_own, x_received, in_a, in_b, in_c, token, out, row_mine, plane, col):
    z = lax.axis_index("bz")
    rows, ni = row_own.shape
    rb, cb = rows // 2, col_own.shape[0]
    rest = in_a.shape[0] - col_own.shape[1] // out.shape[1] * cb
    out[:rest] = (core_own[core_own.shape[0] - rest :] + in_a[:rest]) + (in_b[:rest] + in_c[:rest])
    mine, away = block(z, rb), block(1 - z, rb)
    row_mine[...] = row_own[mine] + x_received[mine]
    turned = row_own[away] + x_received[away]
    out[rest:, :ni] = turned[: rb // 2]
    out[rest:, ni:] = turned[rb // 2 :]
    total = plane_sum[...] + x_received[rows:]
    for part in range(plane.shape[1] // ni):
        plane[:, part * ni : (part + 1) * ni] = total[part : part + 1]
    wide = out.shape[1]
    for part in range(col.shape[1] // wide):
        lanes = slice(part * wide, (part + 1) * wide)
        got = slice(rest + part * cb, rest + (part + 1) * cb)
        col[:, lanes] = (col_own[:, lanes] + in_a[got]) + (in_b[got] + in_c[got])


def write(at, planes, own, other, table, out, buf, sem):
    nb, cb, rows = buf.shape[:3]
    start, steps = planes[0] // cb, (planes[1] - planes[0]) // cb
    nb = min(nb, steps)

    def copy(s, slot):
        return pltpu.make_async_copy(buf.at[slot], out.at[block(start + s, cb), pl.ds(at, rows)], sem.at[slot])

    def step(s, _):
        slot = lax.rem(s, nb)

        @pl.when(s >= nb)
        def _():
            copy(s - nb, slot).wait()

        for c in range(cb):
            row = pl.ds((start + s) * cb + c, 1)
            buf[slot, c] = table[0, row] * own[:rows] + table[1, row] * other[:rows]
        copy(s, slot).start()
        return 0

    lax.fori_loop(0, steps, step, 0)

    def drain(s, _):
        copy(s, lax.rem(s, nb)).wait()
        return 0

    lax.fori_loop(steps - nb, steps, drain, 0)


def write_first(own, other, table, out, token, buf, sem):
    write(0, (0, out.shape[0] - LAST), own, other, table, out, buf, sem)
    token[...] = jnp.zeros_like(token)


def write_rest(own, other, table, core, out, buf, sem):
    write(0, (out.shape[0] - LAST, out.shape[0]), own, other, table, out, buf, sem)


def write_second(own, other, table, row_mine, plane, col, core, out, plane_out, row_out, col_out, buf, sem, row_buf, out_sem):
    rest, ni = buf.shape[2], row_buf.shape[1]
    half = row_buf.shape[0] // 2
    row_buf[:half] = row_mine[:half] + other[rest:, :ni]
    row_buf[half:] = row_mine[half:] + other[rest:, ni:]
    copies = read((plane, row_buf, col), (plane_out, row_out, col_out), out_sem)
    write(out.shape[1] - rest, (0, out.shape[0]), own, other, table, out, buf, sem)
    for c in copies:
        c.wait()


def direct(mesh, slab, plane_test, row_test, col_test, core_planes, core_rows, core_cols):
    nbx, nby, nbz = DIRECT
    _, ni, nj = slab.shape
    k = row_test.shape[1]
    na, nc = core_rows.shape[0], core_planes.shape[0]
    ab, bb = na // nbx, core_cols.shape[0] // nby
    rb, cb = k // (nby * nbz), k // (nbx * nbz)
    cut = FIRST * ab // 8
    rest = ab - cut
    dma = pltpu.SemaphoreType.DMA

    (x_send,) = call(
        others_columns,
        [(bb, ni)],
        (slab, core_cols),
        "hh",
        scratch=[pltpu.VMEM((ni, nj), F32), pltpu.VMEM((bb, nj), F32), dma((2,))],
        cost=(6 * ni * nj * bb, 4 * (ni + bb) * nj),
    )
    x_in = lax.ppermute(x_send, "by", pairs(nby, 1))

    own, row_own, row_away, plane_own, col_terms, col_away, left, table = call(
        own_terms,
        [
            (bb, ni),
            (nbz * rb, ni),
            (nbz * rb, ni),
            (8, ni),
            (nbx * cb, nj),
            (nbx * cb, nj),
            jax.ShapeDtypeStruct((na, 3 * ni), BF16),
            (2, nc, bb),
        ],
        (slab, core_cols, col_test, row_test, plane_test, core_rows, core_planes.T, x_send),
        "hhhhhhhv",
        scratch=[
            pltpu.VMEM((ni, nj), F32),
            pltpu.VMEM((ni, k), F32),
            pltpu.VMEM((1, k), F32),
            pltpu.VMEM((nj, k), F32),
            pltpu.VMEM((bb, nj), F32),
            pltpu.VMEM((na, ni), F32),
            pltpu.VMEM((nbz, nc), F32),
            dma((7,)),
        ],
        cost=(6 * ni * nj * (bb + 2 * k), 4 * (ni * nj + bb * nj + nj * k)),
    )
    right, *sends = call(
        core_first,
        [jax.ShapeDtypeStruct((bb, 3 * ni), BF16)] + [(2 * cut + 8, ni)] * 3,
        (left, own, x_in, plane_own),
        "vvvv",
        cost=(6 * ni * bb * 3 * cut, 4 * ni * bb),
    )
    col_away, *sends = lax.optimization_barrier((col_away, *sends))
    first_in = [lax.ppermute(s, "bx", pairs(nbx, i)) for i, s in zip(FIRST_ORDER, sends)]
    col_in = lax.ppermute(col_away, "bz", pairs(nbz, 1))

    core_own, col_own, *sends = call(
        functools.partial(core_second, cut),
        [(ab, bb), (cb, nj)] + [(rest + cb * nj // bb, bb)] * 3,
        (left, right, col_terms, col_in),
        "vvvv",
        cost=(6 * ni * bb * 4 * ab, 4 * ni * bb),
    )
    second_in = [lax.ppermute(s, "bx", pairs(nbx, i)) for i, s in zip(SECOND_ORDER, sends)]

    first, x_send, plane_sum = call(
        sum_first,
        [(cut, bb), (nbz * rb + 8, ni), (8, ni)],
        (core_own, row_away, plane_own, *first_in),
        "vvvvvv",
    )
    first_other = lax.ppermute(first, "bz", pairs(nbz, 1))
    x_in = lax.ppermute(x_send, "by", pairs(nby, 1))
    early = nc - LAST
    core, token = call(
        write_first,
        [(nc, ab, bb), (8, ni)],
        (first, first_other, table),
        "vvv",
        "hv",
        scratch=[pltpu.VMEM((16, 4, cut, bb), F32), dma((16,))],
        cost=(3 * early * cut * bb, 4 * early * cut * bb),
    )
    second, row_mine, plane, col = call(
        sum_second,
        [(rest + rb // 2, bb), (rb, ni), (1, k), (cb, nj)],
        (core_own, row_own, plane_sum, col_own, x_in, *second_in, token),
        "v" * 9,
    )
    second_other = lax.ppermute(second, "bz", pairs(nbz, 1))
    (core,) = call(
        write_rest,
        [(nc, ab, bb)],
        (first, first_other, table, core),
        "vvvh",
        "h",
        scratch=[pltpu.VMEM((16, 4, cut, bb), F32), dma((16,))],
        cost=(3 * LAST * cut * bb, 4 * LAST * cut * bb),
        input_output_aliases={3: 0},
    )
    core, plane_sketch, row_sketch, col_sketch = call(
        write_second,
        [(nc, ab, bb), (1, k), (rb, ni), (cb, nj)],
        (second, second_other, table, row_mine, plane, col, core),
        "vvvvvvh",
        "hhhh",
        scratch=[pltpu.VMEM((16, 4, rest, bb), F32), dma((16,)), pltpu.VMEM((rb, ni), F32), dma((3,))],
        cost=(3 * nc * rest * bb, 4 * nc * rest * bb),
        input_output_aliases={6: 0},
    )
    return plane_sketch, row_sketch.T, col_sketch.T, core


def stepwise(slab, plane_test, row_test, col_test, core_planes, core_rows, core_cols):
    einsum = functools.partial(jnp.einsum, precision=lax.Precision.HIGHEST)
    by_col = einsum("pij,jr->pir", slab, col_test)
    plane_part = einsum("pir,ir->pr", by_col, row_test)
    row_part = einsum("pir,pr->ir", by_col, plane_test)
    by_row = einsum("pij,ir->pjr", slab, row_test)
    col_part = einsum("pjr,pr->jr", by_row, plane_test)
    plane_sketch = lax.psum(plane_part, ("bx", "by"))
    row_sketch = lax.psum_scatter(row_part, ("by", "bz"), scatter_dimension=1, tiled=True)
    col_sketch = lax.psum_scatter(col_part, ("bx", "bz"), scatter_dimension=1, tiled=True)
    shrunk = einsum("pij,bj->pib", slab, core_cols)
    reduced = lax.psum_scatter(shrunk, "by", scatter_dimension=2, tiled=True)
    partial_value = einsum("pib,ai->pab", reduced, core_rows)
    partial_value = lax.psum_scatter(partial_value, "bx", scatter_dimension=1, tiled=True)
    both = lax.all_gather(partial_value, "bz", axis=0, tiled=True)
    core_sketch = einsum("cp,pab->cab", core_planes, both)
    return plane_sketch, row_sketch, col_sketch, core_sketch


def solution(mesh):
    in_specs = (
        P(("groups", "bz"), "bx", "by"),
        P("bz", None),
        P("bx", None),
        P("by", None),
        P("bz", None),
        P(None, "bx"),
        P(None, "by"),
    )
    out_specs = (
        P(("groups", "bz"), None),
        P(("groups", "bx"), ("by", "bz")),
        P(("groups", "by"), ("bx", "bz")),
        P(("groups", "bz"), "bx", "by"),
    )
    bricks = tuple(mesh.shape[a] for a in ("bx", "by", "bz"))
    body = functools.partial(direct, mesh) if bricks == DIRECT else stepwise
    return jax.shard_map(body, mesh=mesh, in_specs=in_specs, out_specs=out_specs, check_vma=False)
```
